32 devices in a mesh: tm: 4 (over x, core), rep: 8 (over z, y).
Axes of the slice: x: 2, y: 2, z: 4, core: 2. Of those that a mesh axis runs over, the one named last changes fastest.
Arguments:
- samples: bfloat16 [8, 2048, 512], P('rep', 'tm'), may hold values from -5 to 5
- grad_out: bfloat16 [8, 2048, 512], P('rep', 'tm'), may hold values from -4 to 4
- w_conv: bfloat16 [1024, 1024], replicated, may hold values from -0.1875 to 0.1875
- w_res: bfloat16 [512, 512], replicated, may hold values from -0.25 to 0.25
- lengths: int32 [8], P('rep'), may hold values from 512 to 2048
Outputs:
- grad_in: bfloat16 [8, 2048, 512], P('rep', 'tm')
- grad_conv: float32 [1024, 1024], P('tm', 'rep')
- grad_res: float32 [512, 512], P('tm', 'rep')
The draws below stay inside these ranges and needn't reach their ends.
All inputs are finite; a program needn't handle non-finite values.
Results may differ from the reference program's by a relative error of at most 0.015.
Values may be sent and summed in bfloat16 or wider, within the bound.
No kernel may reach another device: no remote copies, remote signals or barrier semaphores. Data moves between devices by JAX's collectives and lax.ppermute only.
A program may use at most 64 MiB of HBM per device.

```python
import jax
import jax.numpy as jnp
from jax import lax

RESIDUAL_WIDTH = 512
TOK_DEV = 512
DILATION_STEP = 256
SEQUENCE_SAMPLES = 2048
SEQS = 8
TOKENS = 16384
N_TM = 4


def place_ends(result, key, smallest, top_value):
    longest = result.shape.index(max(result.shape))
    spots = []
    for shift in (0, 1):
        where = [jax.random.randint(jax.random.fold_in(key, axis), (), 0, length) for axis, length in enumerate(result.shape)]
        where[longest] = (where[longest] + shift) % result.shape[longest]
        spots.append(tuple(where))
    return result.at[spots[0]].set(smallest).at[spots[1]].set(top_value)


def raised(values, key, source, target, blocks, factor):
    def block_of(position):
        return (jnp.arange(values.shape[position]) // (values.shape[position] // blocks)).reshape((-1,) + (1,) * (values.ndim - 1 - position))

    one_side = jax.random.permutation(key, blocks)[block_of(target)]
    far = (block_of(target) + blocks // 2) % blocks
    return jnp.where((block_of(source) == one_side) | (block_of(source) == far), factor * values, values)


def block_scale(rng, dims, shards, smallest, top_value):
    gain = 1.0
    for dim, shards_of in shards:
        draws = jax.random.uniform(jax.random.fold_in(jax.random.fold_in(rng, 6), dim), (shards_of,), jnp.float32, smallest / len(shards), top_value / len(shards))
        gain = gain * jnp.repeat(jnp.exp(draws), dims[dim] // shards_of).reshape((-1,) + (1,) * (len(dims) - 1 - dim))
    return gain


def noise(stream_key, shape, scale, limit, pieces=(), held_as=jnp.bfloat16):
    entries = scale * jax.random.normal(stream_key, shape, jnp.float32)
    if pieces:
        entries = entries * block_scale(stream_key, shape, pieces, -0.22, 0.18)
    return jnp.clip(entries, -limit, limit).astype(held_as)


def bell_draw_with(own_key, extent, spread, limit, cuts, heavy, kind=jnp.bfloat16):
    drawn = spread * jax.random.normal(own_key, extent, jnp.float32)
    if cuts:
        drawn = drawn * block_scale(own_key, extent, cuts, -0.22, 0.18)
    return jnp.clip(raised(drawn, jax.random.fold_in(own_key, 3), *heavy), -limit, limit).astype(kind)


def setup_inputs(seed: int = 0) -> dict:
    streams_of = jax.random.split(jax.random.key(seed), 6)
    return {
        "samples": bell_draw_with(streams_of[0], (SEQS, SEQUENCE_SAMPLES, RESIDUAL_WIDTH), 0.6, 5.0, ((0, 8), (1, 4)), (1, 2, 4, 2.0)),
        "grad_out": noise(streams_of[1], (SEQS, SEQUENCE_SAMPLES, RESIDUAL_WIDTH), 0.5, 4.0, ((0, 8), (1, 4))),
        "w_conv": noise(streams_of[2], (2 * RESIDUAL_WIDTH, 2 * RESIDUAL_WIDTH), (2 * RESIDUAL_WIDTH) ** -0.5, 0.1875),
        "w_res": noise(streams_of[3], (RESIDUAL_WIDTH, RESIDUAL_WIDTH), RESIDUAL_WIDTH ** -0.5, 0.25),
        "lengths": place_ends(jax.random.randint(streams_of[4], (SEQS,), SEQUENCE_SAMPLES // 4, SEQUENCE_SAMPLES + 1), jax.random.fold_in(streams_of[4], 1), SEQUENCE_SAMPLES // 4, SEQUENCE_SAMPLES).astype(jnp.int32),
    }


def gate_backward(inputs, cotangent, in_length, w_conv, w_res):
    channel_count = w_res.shape[0]
    pre_act = jnp.dot(inputs, w_conv, preferred_element_type=jnp.float32)
    tanh_f = jnp.tanh(pre_act[:, :channel_count])
    sig_g = jax.nn.sigmoid(pre_act[:, channel_count:])
    gated = (in_length * tanh_f * sig_g).astype(jnp.bfloat16)
    gated_grad = in_length * jnp.dot(cotangent, w_res.T, preferred_element_type=jnp.float32)
    pre_grad = jnp.concatenate([gated_grad * sig_g * (1.0 - tanh_f * tanh_f),
                                gated_grad * tanh_f * sig_g * (1.0 - sig_g)], 1).astype(jnp.bfloat16)
    return gated, pre_grad


def block_terms(left, right):
    left_blocks = left.reshape(N_TM, TOK_DEV, left.shape[1]).astype(jnp.float32)
    right_blocks = right.reshape(N_TM, TOK_DEV, right.shape[1]).astype(jnp.float32)
    terms = jnp.einsum('btk,btn->bkn', left_blocks, right_blocks).astype(jnp.bfloat16)
    terms = lax.optimization_barrier(terms)
    return jnp.sum(terms.astype(jnp.float32), axis=0)


def reference(samples, grad_out, w_conv, w_res, lengths):
    def one_sequence(carry, item):
        sequence_rows, cotangent, seq_len = item
        prior_samples = jnp.concatenate([jnp.zeros((DILATION_STEP, RESIDUAL_WIDTH), jnp.bfloat16), sequence_rows[:SEQUENCE_SAMPLES - DILATION_STEP]], 0)
        inputs = jnp.concatenate([prior_samples, sequence_rows], 1)
        in_length = (jnp.arange(SEQUENCE_SAMPLES) < seq_len).astype(jnp.float32)[:, None]
        gated, pre_grad = gate_backward(inputs, cotangent, in_length, w_conv, w_res)
        input_gradient = jnp.dot(pre_grad, w_conv.T, preferred_element_type=jnp.float32)
        delayed_gradient = jnp.concatenate([input_gradient[DILATION_STEP:, :RESIDUAL_WIDTH], jnp.zeros((DILATION_STEP, RESIDUAL_WIDTH), jnp.float32)], 0)
        grad_rows = (cotangent.astype(jnp.float32) + input_gradient[:, RESIDUAL_WIDTH:] + delayed_gradient).astype(jnp.bfloat16)
        sum_conv = carry[0] + block_terms(inputs, pre_grad)
        sum_res = carry[1] + block_terms(gated, cotangent)
        return (sum_conv, sum_res), grad_rows

    start = (jnp.zeros((2 * RESIDUAL_WIDTH, 2 * RESIDUAL_WIDTH), jnp.float32), jnp.zeros((RESIDUAL_WIDTH, RESIDUAL_WIDTH), jnp.float32))
    (sum_conv, sum_res), grad_in = lax.scan(one_sequence, start, (samples, grad_out, lengths))
    grad_scale = float(TOKENS) ** -0.5
    return grad_in, sum_conv * grad_scale, sum_res * grad_scale
```

```python
import functools

import jax
import jax.numpy as jnp
from jax import lax
from jax.experimental import pallas as pl
from jax.experimental.pallas import tpu as pltpu
from jax.sharding import PartitionSpec as P

DILATION_STEP = 256
VMEM_GRANT = 32 * 1024 * 1024
F32, BF16 = jnp.float32, jnp.bfloat16


def dot(left, right):
    return jnp.dot(left, right, preferred_element_type=F32)


def dot_nt(left, right):
    return lax.dot_general(left, right, (((1,), (1,)), ((), ())), preferred_element_type=F32)


def gates(pre_act, gated_grad, in_length):
    channels = pre_act.shape[1] // 2
    tanh_f = jnp.tanh(pre_act[:, :channels])
    sig_g = 0.5 + 0.5 * jnp.tanh(0.5 * pre_act[:, channels:])
    both = tanh_f * sig_g
    gated = (in_length * both).astype(BF16)
    pre_f = (gated_grad * (sig_g * (1.0 - tanh_f * tanh_f))).astype(BF16)
    pre_g = (gated_grad * (both * (1.0 - sig_g))).astype(BF16)
    return gated, pre_f, pre_g


def length_mask(lengths_ref, first_row, rows, total_rows):
    start = lax.axis_index("tm") * total_rows + first_row
    at = start + lax.broadcasted_iota(jnp.int32, (rows, 1), 0)
    return (at < lengths_ref[0]).astype(F32)


def local_kernel(lengths_ref, x_ref, c_ref, wc_ref, wr_ref, xt_ref, ct_ref, cur_ref, gg_ref, pg_ref, ga_ref):
    rows, channels = x_ref.shape
    step = DILATION_STEP
    gated_grad = dot_nt(c_ref[...], wr_ref[...])
    gg_ref[...] = gated_grad[:step] * length_mask(lengths_ref, 0, step, rows)
    cur = dot(x_ref[...], wc_ref[channels:, :])
    cur_ref[...] = cur[:step]
    pre_act = cur[step:] + dot(x_ref[: rows - step, :], wc_ref[:channels, :])
    mask = length_mask(lengths_ref, step, rows - step, rows)
    gated, pre_f, pre_g = gates(pre_act, gated_grad[step:] * mask, mask)
    ga_ref[...] = gated
    pg_ref[:, :channels] = pre_f
    pg_ref[:, channels:] = pre_g
    xt_ref[...] = x_ref[...].T.reshape(xt_ref.shape)
    ct_ref[...] = c_ref[...].T


def block_products(parity, xt_ref, ht_ref, ct_ref, pg_ref, gb_ref, out_ref):
    halves, reps, height, lanes = out_ref.shape
    blocks, h, rows = xt_ref.shape
    back = ht_ref.shape[2]
    columns = pg_ref.shape[1]
    per_tap = blocks // 2
    earlier = [
        jnp.concatenate([ht_ref[2 * i + parity], xt_ref[2 * i + parity][:, : rows - back]], 1)
        for i in range(per_tap)
    ]
    current = [xt_ref[2 * i + parity] for i in range(per_tap)]
    left = jnp.concatenate(earlier + current, 0)
    wide = min(256, columns)
    for j in range(0, columns, wide):
        term = dot(left, pg_ref[:, j : j + wide]).astype(BF16)
        for t in range(halves):
            for k in range(0, wide, lanes):
                out_ref[t, (j + k) // lanes, :h, :] = term[t * h : (t + 1) * h, k : k + lanes]
    right = jnp.concatenate([gb_ref[2 * t + parity] for t in range(halves)], 1)
    term = dot(ct_ref[...], right).astype(BF16)
    low = height - h
    for t in range(halves):
        for r in range(reps):
            out_ref[t, r, h:, :] = term[r * low : (r + 1) * low, t * lanes : (t + 1) * lanes]


def partner_kernel(
    lengths_ref, halo_ref, wc_ref, xt_ref, ct_ref, cur_ref, gg_ref, pgh_ref, gah_ref,
    pg_ref, gb_ref, ht_ref, out_ref,
):
    step, channels = halo_ref.shape
    rows = pg_ref.shape[0]
    lanes = gb_ref.shape[2]
    pre_act = cur_ref[...] + dot(halo_ref[...], wc_ref[:channels, :])
    mask = length_mask(lengths_ref, 0, step, rows)
    gated, pre_f, pre_g = gates(pre_act, gg_ref[...], mask)
    pg_ref[:step, :channels] = pre_f
    pg_ref[:step, channels:] = pre_g
    pg_ref[step:, :] = pgh_ref[...]
    for t in range(gb_ref.shape[0]):
        gb_ref[t, :step, :] = gated[:, t * lanes : (t + 1) * lanes]
        gb_ref[t, step:, :] = gah_ref[:, t * lanes : (t + 1) * lanes]
    ht_ref[...] = halo_ref[...].T.reshape(ht_ref.shape)
    parity = 1 - lax.rem(lax.axis_index("tm"), 2)
    block_products(parity, xt_ref, ht_ref, ct_ref, pg_ref, gb_ref, out_ref)


def own_kernel(xt_ref, ht_ref, ct_ref, pg_ref, gb_ref, out_ref):
    parity = lax.rem(lax.axis_index("tm"), 2)
    block_products(parity, xt_ref, ht_ref, ct_ref, pg_ref, gb_ref, out_ref)


def input_kernel(pg_ref, wc_ref, c_ref, lo_ref, hi_ref, back_ref):
    step = DILATION_STEP
    rows, channels = c_ref.shape
    current = dot_nt(pg_ref[...], wc_ref[channels:, :]) + c_ref[...].astype(F32)
    earlier = dot_nt(pg_ref[...], wc_ref[:channels, :])
    back_ref[...] = earlier[:step].astype(BF16)
    lo_ref[...] = (current[: rows - step] + earlier[step:]).astype(BF16)
    hi_ref[...] = current[rows - step :]


def split_kernel(count_x, count_z, got_ref, kept_ref, *outs):
    halves, reps, height, lanes = got_ref.shape
    x = lax.axis_index("tm") // 2
    rep = lax.axis_index("rep")
    z, y = rep // 2, lax.rem(rep, 2)
    wide = outs[0].shape[1]
    for d in range(2 * count_x):
        to_x, to_y = x ^ (d // 2), y ^ (d % 2)
        for to_z in range(count_z):
            r = 2 * to_z + to_y
            part = got_ref[to_x, r, :wide, :].astype(F32) + kept_ref[to_x, r, :wide, :].astype(F32)
            outs[d][to_z] = part.astype(BF16)
    if wide == height:
        return
    for d in range(count_z):
        to_z = z ^ d
        for to_x in range(count_x):
            for to_y in range(2):
                r = 2 * to_z + to_y
                part = got_ref[to_x, r, wide:, :].astype(F32) + kept_ref[to_x, r, wide:, :].astype(F32)
                outs[2 * count_x + d][2 * to_x + to_y] = part.astype(BF16)


def total_of(refs, index):
    total = refs[0][index].astype(F32)
    for ref in refs[1:]:
        total = total + ref[index].astype(F32)
    return total


def plane_kernel(count_x, count_z, *refs):
    parts, outs = refs[: 2 * count_x], refs[2 * count_x :]
    z = lax.axis_index("rep") // 2
    for d in range(count_z):
        outs[d][...] = total_of(parts, z ^ d).astype(BF16)


def line_kernel(count_x, count_z, *refs):
    parts, outs = refs[:count_z], refs[count_z:]
    x = lax.axis_index("tm") // 2
    y = lax.rem(lax.axis_index("rep"), 2)
    for d in range(2 * count_x):
        outs[d][...] = total_of(parts, 2 * (x ^ (d // 2)) + (y ^ (d % 2))).astype(BF16)


def final_kernel(scale, count_first, *refs):
    first, second, (conv_ref, res_ref) = refs[:count_first], refs[count_first:-2], refs[-2:]
    total = total_of(first, ...)
    if second:
        total = jnp.concatenate([total, total_of(second, ...)], 0)
    total = total * scale
    height = conv_ref.shape[0]
    conv_ref[...] = total[:height]
    res_ref[...] = total[height:]


def call(kernel, out_shapes, flops, *args, name):
    specs = [
        pl.BlockSpec(memory_space=pltpu.SMEM) if a.dtype == jnp.int32 else pl.BlockSpec(memory_space=pltpu.VMEM)
        for a in args
    ]
    out_shape = [jax.ShapeDtypeStruct(shape, kind) for shape, kind in out_shapes]
    moved = sum(a.size * a.dtype.itemsize for a in list(args) + out_shape)
    return pl.pallas_call(
        kernel,
        out_shape=out_shape,
        in_specs=specs,
        out_specs=[pl.BlockSpec(memory_space=pltpu.VMEM)] * len(out_shape),
        cost_estimate=pl.CostEstimate(flops=int(flops), bytes_accessed=int(moved), transcendentals=0),
        compiler_params=pltpu.CompilerParams(vmem_limit_bytes=VMEM_GRANT),
        name=name,
    )(*args)


def body(samples, grad_out, w_conv, w_res, lengths):
    x, cot = samples[0], grad_out[0]
    rows, channels = x.shape
    step = DILATION_STEP
    tms, reps = lax.axis_size("tm"), lax.axis_size("rep")
    halves, count_z = tms // 2, reps // 2
    h, low = 2 * channels // tms, channels // reps
    lanes = channels // tms
    height = h + low
    devices = tms * reps

    def swap(array, mask):
        return lax.ppermute(array, ("tm", "rep"), [(i, i ^ mask) for i in range(devices)])

    halo = lax.ppermute(x[rows - step :], "tm", [(i, i + 1) for i in range(tms - 1)])
    xt, ct, cur, gg, pgh, gah = call(
        local_kernel,
        [
            ((tms // 2, h, rows), BF16), ((channels, rows), BF16), ((step, 2 * channels), F32),
            ((step, channels), F32), ((rows - step, 2 * channels), BF16), ((rows - step, channels), BF16),
        ],
        2 * rows * channels * channels * 4,
        lengths, x, cot, w_conv, w_res, name="local",
    )
    term = ((halves, reps, height, lanes), BF16)
    pg, gb, ht, theirs = call(
        partner_kernel,
        [((rows, 2 * channels), BF16), ((tms, rows, lanes), BF16), ((tms // 2, h, step), BF16), term],
        2 * rows * channels * channels * 4,
        lengths, halo, w_conv, xt, ct, cur, gg, pgh, gah, name="partner",
    )
    got = swap(theirs, reps)
    (mine,) = call(own_kernel, [term], 2 * rows * channels * channels * 3, xt, ht, ct, pg, gb, name="own")

    narrow = (height * 6 // 17) // 16 * 16
    wide = height - narrow
    plane = ((count_z, wide, lanes), BF16)
    line = ((2 * halves, narrow, lanes), BF16)
    parts = call(
        functools.partial(split_kernel, halves, count_z),
        [plane] * (2 * halves) + [line] * count_z,
        term[0][0] * reps * height * lanes,
        got, mine, name="split",
    )
    plane_masks = [(d // 2) * 2 * reps + d % 2 for d in range(2 * halves)]
    line_masks = [2 * d for d in range(count_z)]
    planes = [swap(p, m) if m else p for p, m in zip(parts[: 2 * halves], plane_masks)]
    lines = [swap(p, m) if m else p for p, m in zip(parts[2 * halves :], line_masks)]
    lo, hi, back = call(
        input_kernel,
        [((rows - step, channels), BF16), ((step, channels), F32), ((step, channels), BF16)],
        2 * rows * channels * channels * 4,
        pg, w_conv, cot, name="input",
    )
    parts = call(
        functools.partial(plane_kernel, halves, count_z),
        [(plane[0][1:], BF16)] * count_z, height * lanes * 16, *planes, name="plane",
    )
    firsts = [swap(p, m) if m else p for p, m in zip(parts, line_masks)]
    parts = call(
        functools.partial(line_kernel, halves, count_z),
        [(line[0][1:], BF16)] * (2 * halves), height * lanes * 16, *lines, name="line",
    )
    seconds = [swap(p, m) if m else p for p, m in zip(parts, plane_masks)]
    back = lax.ppermute(back, "tm", [(i + 1, i) for i in range(tms - 1)])
    grad_rows = jnp.concatenate([lo, (hi + back.astype(F32)).astype(BF16)], 0)
    scale = float(rows * devices) ** (-0.5)
    conv, res = call(
        functools.partial(final_kernel, scale, count_z),
        [((h, lanes), F32), ((low, lanes), F32)], height * lanes * 8, *firsts, *seconds, name="final",
    )
    return grad_rows[None], conv, res.T


def solution(mesh):
    return jax.shard_map(
        body,
        mesh=mesh,
        in_specs=(P("rep", "tm", None), P("rep", "tm", None), P(), P(), P("rep")),
        out_specs=(P("rep", "tm", None), P("tm", "rep"), P("tm", "rep")),
        check_vma=False,
    )
```

```python
import functools

import jax
import jax.numpy as jnp
from jax import lax
from jax.experimental import pallas as pl
from jax.experimental.pallas import tpu as pltpu
from jax.sharding import PartitionSpec as P

DILATION_STEP = 256
VMEM_GRANT = 32 * 1024 * 1024
F32, BF16 = jnp.float32, jnp.bfloat16


def dot(left, right):
    return jnp.dot(left, right, preferred_element_type=F32)


def dot_nt(left, right):
    return lax.dot_general(left, right, (((1,), (1,)), ((), ())), preferred_element_type=F32)


def gates(pre_act, gated_grad, in_length):
    channels = pre_act.shape[1] // 2
    tanh_f = jnp.tanh(pre_act[:, :channels])
    sig_g = 0.5 + 0.5 * jnp.tanh(0.5 * pre_act[:, channels:])
    both = tanh_f * sig_g
    gated = (in_length * both).astype(BF16)
    pre_f = (gated_grad * (sig_g * (1.0 - tanh_f * tanh_f))).astype(BF16)
    pre_g = (gated_grad * (both * (1.0 - sig_g))).astype(BF16)
    return gated, pre_f, pre_g


def length_mask(lengths_ref, first_row, rows, total_rows):
    start = lax.axis_index("tm") * total_rows + first_row
    at = start + lax.broadcasted_iota(jnp.int32, (rows, 1), 0)
    return (at < lengths_ref[0]).astype(F32)


def local_kernel(
    lengths_ref, x_hbm, c_hbm, wc_hbm, wr_hbm,
    xt_ref, ct_ref, cur_ref, gg_ref, pg_ref, gb_ref, wc_ref, c_ref, x_ref, wr_ref, sems,
):
    rows, channels = x_ref.shape
    step = DILATION_STEP
    lanes = gb_ref.shape[2]
    low, high = pl.ds(0, channels), pl.ds(channels, channels)
    copies = [
        pltpu.make_async_copy(source, target, sems.at[i])
        for i, (source, target) in enumerate(
            [
                (x_hbm, x_ref), (wc_hbm.at[high], wc_ref.at[high]), (wc_hbm.at[low], wc_ref.at[low]),
                (c_hbm, c_ref), (wr_hbm, wr_ref),
            ]
        )
    ]
    for copy in copies:
        copy.start()
    copies[0].wait()
    xt_ref[...] = x_ref[...].T.reshape(xt_ref.shape)
    copies[1].wait()
    cur_ref[...] = dot(x_ref[:step, :], wc_ref[channels:, :])
    pre_act = dot(x_ref[step:, :], wc_ref[channels:, :])
    copies[2].wait()
    pre_act = pre_act + dot(x_ref[: rows - step, :], wc_ref[:channels, :])
    copies[3].wait()
    copies[4].wait()
    gated_grad = dot_nt(c_ref[...], wr_ref[...])
    gg_ref[...] = gated_grad[:step] * length_mask(lengths_ref, 0, step, rows)
    mask = length_mask(lengths_ref, step, rows - step, rows)
    gated, pre_f, pre_g = gates(pre_act, gated_grad[step:] * mask, mask)
    for t in range(gb_ref.shape[0]):
        gb_ref[t, step:, :] = gated[:, t * lanes : (t + 1) * lanes]
    pg_ref[step:, :channels] = pre_f
    pg_ref[step:, channels:] = pre_g
    ct_ref[...] = c_ref[...].T


def block_products(parity, xt_ref, ht_ref, ct_ref, pg_ref, gb_ref, out_ref):
    halves, reps, height, lanes = out_ref.shape
    blocks, h, rows = xt_ref.shape
    back = ht_ref.shape[2]
    columns = pg_ref.shape[1]
    per_tap = blocks // 2
    earlier = [
        jnp.concatenate([ht_ref[2 * i + parity], xt_ref[2 * i + parity][:, : rows - back]], 1)
        for i in range(per_tap)
    ]
    current = [xt_ref[2 * i + parity] for i in range(per_tap)]
    left = jnp.concatenate(earlier + current, 0)
    wide = min(256, columns)
    for j in range(0, columns, wide):
        term = dot(left, pg_ref[:, j : j + wide]).astype(BF16)
        for t in range(halves):
            for k in range(0, wide, lanes):
                out_ref[t, (j + k) // lanes, :h, :] = term[t * h : (t + 1) * h, k : k + lanes]
    right = jnp.concatenate([gb_ref[2 * t + parity] for t in range(halves)], 1)
    term = dot(ct_ref[...], right).astype(BF16)
    low = height - h
    for t in range(halves):
        for r in range(reps):
            out_ref[t, r, h:, :] = term[r * low : (r + 1) * low, t * lanes : (t + 1) * lanes]


def partner_kernel(
    lengths_ref, halo_ref, wc_ref, xt_ref, ct_ref, cur_ref, gg_ref, pg_in, gb_in,
    pg_ref, gb_ref, ht_ref, out_ref,
):
    step, channels = halo_ref.shape
    rows = pg_ref.shape[0]
    lanes = gb_ref.shape[2]
    halo = jnp.where(lax.axis_index("tm") > 0, halo_ref[...], jnp.zeros_like(halo_ref))
    pre_act = cur_ref[...] + dot(halo, wc_ref[:channels, :])
    mask = length_mask(lengths_ref, 0, step, rows)
    gated, pre_f, pre_g = gates(pre_act, gg_ref[...], mask)
    pg_ref[:step, :channels] = pre_f
    pg_ref[:step, channels:] = pre_g
    for t in range(gb_ref.shape[0]):
        gb_ref[t, :step, :] = gated[:, t * lanes : (t + 1) * lanes]
    ht_ref[...] = halo.T.reshape(ht_ref.shape)
    parity = 1 - lax.rem(lax.axis_index("tm"), 2)
    block_products(parity, xt_ref, ht_ref, ct_ref, pg_ref, gb_ref, out_ref)


def own_kernel(xt_ref, ht_ref, ct_ref, pg_ref, gb_ref, out_ref):
    parity = lax.rem(lax.axis_index("tm"), 2)
    block_products(parity, xt_ref, ht_ref, ct_ref, pg_ref, gb_ref, out_ref)


def back_kernel(pg_ref, wc_ref, back_ref):
    step, channels = back_ref.shape
    back_ref[...] = dot_nt(pg_ref[:step, :], wc_ref[:channels, :]).astype(BF16)


def input_kernel(pg_ref, wc_ref, c_ref, arrived_ref, out_ref):
    step = DILATION_STEP
    rows, channels = c_ref.shape
    current = dot_nt(pg_ref[...], wc_ref[channels:, :]) + c_ref[...].astype(F32)
    earlier = dot_nt(pg_ref[step:, :], wc_ref[:channels, :])
    out_ref[: rows - step, :] = (current[: rows - step] + earlier).astype(BF16)
    arrived = jnp.where(lax.axis_index("tm") < lax.axis_size("tm") - 1, arrived_ref[...].astype(F32), 0.0)
    out_ref[rows - step :, :] = (current[rows - step :] + arrived).astype(BF16)


def split_kernel(count_x, count_z, got_ref, kept_ref, *outs):
    x = lax.axis_index("tm") // 2
    rep = lax.axis_index("rep")
    y = lax.rem(rep, 2)
    for d, out in enumerate(outs):
        to_x, to_y = x ^ (d // 2), y ^ (d % 2)
        for to_z in range(count_z):
            r = 2 * to_z + to_y
            out[to_z] = (got_ref[to_x, r].astype(F32) + kept_ref[to_x, r].astype(F32)).astype(BF16)


def total_of(refs, index):
    total = refs[0][index].astype(F32)
    for ref in refs[1:]:
        total = total + ref[index].astype(F32)
    return total


def plane_kernel(count_x, count_z, *refs):
    parts, outs = refs[: 2 * count_x], refs[2 * count_x :]
    z = lax.axis_index("rep") // 2
    for d in range(count_z):
        outs[d][...] = total_of(parts, z ^ d).astype(BF16)


def final_kernel(scale, *refs):
    parts, (conv_ref, res_ref) = refs[:-2], refs[-2:]
    total = total_of(parts, ...) * scale
    height = conv_ref.shape[0]
    conv_ref[...] = total[:height]
    res_ref[...] = total[height:]


def call(kernel, out_shapes, flops, *args, name, in_hbm=(), scratch=(), aliases=None):
    def spec(index, a):
        if index in in_hbm:
            return pl.BlockSpec(memory_space=pltpu.HBM)
        return pl.BlockSpec(memory_space=pltpu.SMEM if a.dtype == jnp.int32 else pltpu.VMEM)

    args = [pltpu.with_memory_space_constraint(a, pltpu.HBM) if i in in_hbm else a for i, a in enumerate(args)]
    out_shape = [jax.ShapeDtypeStruct(shape, kind) for shape, kind in out_shapes]
    moved = sum(a.size * a.dtype.itemsize for a in list(args) + out_shape)
    return pl.pallas_call(
        kernel,
        out_shape=out_shape,
        in_specs=[spec(i, a) for i, a in enumerate(args)],
        out_specs=[pl.BlockSpec(memory_space=pltpu.VMEM)] * len(out_shape),
        scratch_shapes=list(scratch),
        input_output_aliases=aliases or {},
        cost_estimate=pl.CostEstimate(flops=int(flops), bytes_accessed=int(moved), transcendentals=0),
        compiler_params=pltpu.CompilerParams(vmem_limit_bytes=VMEM_GRANT),
        name=name,
    )(*args)


def after(array, other):
    return lax.optimization_barrier((array, other))[0]


def body(samples, grad_out, w_conv, w_res, lengths):
    x, cot = samples[0], grad_out[0]
    rows, channels = x.shape
    step = DILATION_STEP
    tms, reps = lax.axis_size("tm"), lax.axis_size("rep")
    halves, count_z = tms // 2, reps // 2
    h, low = 2 * channels // tms, channels // reps
    lanes = channels // tms
    height = h + low
    devices = tms * reps
    product = 2 * rows * channels * channels

    def swap(array, mask):
        return lax.ppermute(array, ("tm", "rep"), [(i, i ^ mask) for i in range(devices)])

    halo = lax.ppermute(x[rows - step :], "tm", [(i, (i + 1) % tms) for i in range(tms)])
    whole_pg, whole_gb = ((rows, 2 * channels), BF16), ((tms, rows, lanes), BF16)
    xt, ct, cur, gg, pg, gb, wc, c = call(
        local_kernel,
        [
            ((tms // 2, h, rows), BF16), ((channels, rows), BF16), ((step, 2 * channels), F32),
            ((step, channels), F32), whole_pg, whole_gb, (w_conv.shape, BF16), (cot.shape, BF16),
        ],
        product * 4, lengths, x, cot, w_conv, w_res, name="local", in_hbm=(1, 2, 3, 4),
        scratch=[pltpu.VMEM(x.shape, BF16), pltpu.VMEM(w_res.shape, BF16), pltpu.SemaphoreType.DMA((5,))],
    )
    term = ((halves, reps, height, lanes), BF16)
    pg, gb, ht, theirs = call(
        partner_kernel,
        [whole_pg, whole_gb, ((tms // 2, h, step), BF16), term],
        product * 4, lengths, halo, wc, xt, ct, cur, gg, pg, gb, name="partner", aliases={7: 0, 8: 1},
    )
    got = swap(theirs, reps)
    (mine,) = call(own_kernel, [term], product * 3, xt, ht, ct, pg, gb, name="own")
    pg, mine = lax.optimization_barrier((pg, mine))
    (back,) = call(back_kernel, [((step, channels), BF16)], product, pg, wc, name="back")
    arrived = lax.ppermute(back, "tm", [((i + 1) % tms, i) for i in range(tms)])

    plane = ((count_z, height, lanes), BF16)
    parts = call(
        functools.partial(split_kernel, halves, count_z),
        [plane] * (2 * halves),
        term[0][0] * reps * height * lanes,
        got, mine, name="split",
    )
    plane_masks = [(d // 2) * 2 * reps + d % 2 for d in range(2 * halves)]
    line_masks = [2 * d for d in range(count_z)]
    planes = [swap(p, m) if m else p for p, m in zip(parts[: 2 * halves], plane_masks)]
    (grad_in,) = call(
        input_kernel, [((rows, channels), BF16)], product * 4, after(pg, planes[1]), wc, c, arrived, name="input",
    )
    parts = call(
        functools.partial(plane_kernel, halves, count_z),
        [(plane[0][1:], BF16)] * count_z, height * lanes * 16, *planes, name="plane",
    )
    firsts = list(parts)
    for d in list(range(2, count_z)) + [1]:
        firsts[d] = swap(firsts[d], line_masks[d])
    scale = float(rows * devices) ** (-0.5)
    conv, res = call(
        functools.partial(final_kernel, scale),
        [((h, lanes), F32), ((low, lanes), F32)], height * lanes * 8, *firsts[2:], *firsts[:2], name="final",
    )
    return grad_in[None], conv, res.T


def solution(mesh):
    return jax.shard_map(
        body,
        mesh=mesh,
        in_specs=(P("rep", "tm", None), P("rep", "tm", None), P(), P(), P("rep")),
        out_specs=(P("rep", "tm", None), P("tm", "rep"), P("tm", "rep")),
        check_vma=False,
    )
```

```python
import functools

import jax
import jax.numpy as jnp
from jax import lax
from jax.experimental import pallas as pl
from jax.experimental.pallas import tpu as pltpu
from jax.sharding import PartitionSpec as P

DILATION_STEP = 256
VMEM_GRANT = 32 * 1024 * 1024
FIRST_CHUNK = 10
F32, BF16 = jnp.float32, jnp.bfloat16


def dot(left, right):
    return jnp.dot(left, right, preferred_element_type=F32)


def dot_nt(left, right):
    return lax.dot_general(left, right, (((1,), (1,)), ((), ())), preferred_element_type=F32)


def gates(pre_act, gated_grad, in_length):
    channels = pre_act.shape[1] // 2
    tanh_f = jnp.tanh(pre_act[:, :channels])
    sig_g = 0.5 + 0.5 * jnp.tanh(0.5 * pre_act[:, channels:])
    both = tanh_f * sig_g
    gated = (in_length * both).astype(BF16)
    pre_f = (gated_grad * (sig_g * (1.0 - tanh_f * tanh_f))).astype(BF16)
    pre_g = (gated_grad * (both * (1.0 - sig_g))).astype(BF16)
    return gated, pre_f, pre_g


def length_mask(lengths_ref, first_row, rows, total_rows):
    start = lax.axis_index("tm") * total_rows + first_row
    at = start + lax.broadcasted_iota(jnp.int32, (rows, 1), 0)
    return (at < lengths_ref[0]).astype(F32)


def local_kernel(
    lengths_ref, x_hbm, c_hbm, wc_hbm, wr_hbm,
    xt_ref, ct_ref, cur_ref, gg_ref, pg_ref, gb_ref, wc_ref, c_ref, x_ref, wr_ref, sems,
):
    rows, channels = x_ref.shape
    step = DILATION_STEP
    lanes = gb_ref.shape[2]
    low, high = pl.ds(0, channels), pl.ds(channels, channels)
    copies = [
        pltpu.make_async_copy(source, target, sems.at[i])
        for i, (source, target) in enumerate(
            [
                (x_hbm, x_ref), (wc_hbm.at[high], wc_ref.at[high]), (wc_hbm.at[low], wc_ref.at[low]),
                (c_hbm, c_ref), (wr_hbm, wr_ref),
            ]
        )
    ]
    for copy in copies:
        copy.start()
    copies[0].wait()
    xt_ref[...] = x_ref[...].T.reshape(xt_ref.shape)
    copies[1].wait()
    cur_ref[...] = dot(x_ref[:step, :], wc_ref[channels:, :])
    pre_act = dot(x_ref[step:, :], wc_ref[channels:, :])
    copies[2].wait()
    pre_act = pre_act + dot(x_ref[: rows - step, :], wc_ref[:channels, :])
    copies[3].wait()
    copies[4].wait()
    gated_grad = dot_nt(c_ref[...], wr_ref[...])
    gg_ref[...] = gated_grad[:step] * length_mask(lengths_ref, 0, step, rows)
    mask = length_mask(lengths_ref, step, rows - step, rows)
    gated, pre_f, pre_g = gates(pre_act, gated_grad[step:] * mask, mask)
    for t in range(gb_ref.shape[0]):
        gb_ref[t, step:, :] = gated[:, t * lanes : (t + 1) * lanes]
    pg_ref[step:, :channels] = pre_f
    pg_ref[step:, channels:] = pre_g
    ct_ref[...] = c_ref[...].T


def block_products(first, parity, xt_ref, ht_ref, ct_ref, pg_ref, gb_ref, out_ref):
    halves, reps, size, lanes = out_ref.shape
    blocks, h, rows = xt_ref.shape
    back = ht_ref.shape[2]
    columns, channels = pg_ref.shape[1], ct_ref.shape[0]
    low, last = channels // reps, first + size
    count = min(last, h) - first
    if count > 0:
        some = pl.ds(first, count)
        picked = [2 * i + parity for i in range(blocks // 2)]
        earlier = [jnp.concatenate([ht_ref[i, some], xt_ref[i, some, : rows - back]], 1) for i in picked]
        left = jnp.concatenate(earlier + [xt_ref[i, some] for i in picked], 0)
        wide = min(256, columns)
        for j in range(0, columns, wide):
            term = dot(left, pg_ref[:, j : j + wide]).astype(BF16)
            for t in range(halves):
                for k in range(0, wide, lanes):
                    out_ref[t, (j + k) // lanes, :count, :] = term[t * count : (t + 1) * count, k : k + lanes]
    count = max(count, 0)
    if last > h:
        skip, part = max(first, h) - h, size - count
        right = jnp.concatenate([gb_ref[2 * t + parity] for t in range(halves)], 1)
        if part == low:
            left = ct_ref[...]
        else:
            left = jnp.concatenate([ct_ref[pl.ds(r * low + skip, part), :] for r in range(reps)], 0)
        term = dot(left, right).astype(BF16)
        for t in range(halves):
            for r in range(reps):
                out_ref[t, r, count:, :] = term[r * part : (r + 1) * part, t * lanes : (t + 1) * lanes]


def partner_kernel(
    first, lengths_ref, halo_ref, wc_ref, xt_ref, ct_ref, cur_ref, gg_ref, pg_in, gb_in,
    pg_ref, gb_ref, ht_ref, out_ref,
):
    step, channels = halo_ref.shape
    rows = pg_ref.shape[0]
    lanes = gb_ref.shape[2]
    halo = jnp.where(lax.axis_index("tm") > 0, halo_ref[...], jnp.zeros_like(halo_ref))
    pre_act = cur_ref[...] + dot(halo, wc_ref[:channels, :])
    mask = length_mask(lengths_ref, 0, step, rows)
    gated, pre_f, pre_g = gates(pre_act, gg_ref[...], mask)
    pg_ref[:step, :channels] = pre_f
    pg_ref[:step, channels:] = pre_g
    for t in range(gb_ref.shape[0]):
        gb_ref[t, :step, :] = gated[:, t * lanes : (t + 1) * lanes]
    ht_ref[...] = halo.T.reshape(ht_ref.shape)
    parity = 1 - lax.rem(lax.axis_index("tm"), 2)
    block_products(first, parity, xt_ref, ht_ref, ct_ref, pg_ref, gb_ref, out_ref)


def terms_kernel(first, away, xt_ref, ht_ref, ct_ref, pg_ref, gb_ref, out_ref):
    parity = lax.rem(lax.axis_index("tm") + away, 2)
    block_products(first, parity, xt_ref, ht_ref, ct_ref, pg_ref, gb_ref, out_ref)


def back_kernel(pg_ref, wc_ref, back_ref):
    step, channels = back_ref.shape
    back_ref[...] = dot_nt(pg_ref[:step, :], wc_ref[:channels, :]).astype(BF16)


def input_kernel(pg_ref, wc_ref, c_ref, lo_ref, hi_ref):
    step = DILATION_STEP
    rows, channels = c_ref.shape
    current = dot_nt(pg_ref[...], wc_ref[channels:, :]) + c_ref[...].astype(F32)
    earlier = dot_nt(pg_ref[step:, :], wc_ref[:channels, :])
    lo_ref[...] = (current[: rows - step] + earlier).astype(BF16)
    hi_ref[...] = current[rows - step :]


def rows_kernel(lo_ref, hi_ref, arrived_ref, out_ref):
    count = lo_ref.shape[0]
    arrived = jnp.where(lax.axis_index("tm") < lax.axis_size("tm") - 1, arrived_ref[...].astype(F32), 0.0)
    out_ref[:count, :] = lo_ref[...]
    out_ref[count:, :] = (hi_ref[...] + arrived).astype(BF16)


def coordinates(count_z):
    tm, rep = lax.axis_index("tm"), lax.axis_index("rep")
    return lax.rem(tm, 2), lax.rem(tm // 2, 2), lax.rem(rep, 2), (tm // 4) * count_z + rep // 2


def split_kernel(count_z, got_ref, kept_ref, stay_ref, send_ref):
    core, x, y, _ = coordinates(count_z)
    for s, out in enumerate((stay_ref, send_ref)):
        for j in range(out.shape[0]):
            far, other = j // 2, j % 2
            to_x = jnp.where(core == 0, x ^ s, other)
            to_y = jnp.where(core == 0, other, y ^ s)
            t, r = 2 * (far // count_z) + to_x, 2 * (far % count_z) + to_y
            out[j] = (got_ref[t, r].astype(F32) + kept_ref[t, r].astype(F32)).astype(BF16)


def half_kernel(count_z, got_ref, kept_ref, stay_ref, send_ref):
    core, x, y, _ = coordinates(count_z)
    mine = jnp.where(core == 0, y, x)
    for s, out in enumerate((stay_ref, send_ref)):
        for far in range(out.shape[0]):
            j = 2 * far + (mine ^ s)
            out[far] = (got_ref[j].astype(F32) + kept_ref[j].astype(F32)).astype(BF16)


def far_kernel(count_z, *refs):
    me = coordinates(count_z)[3]
    chunks = len(refs) - far_count(refs)
    ins, outs = refs[:chunks], refs[chunks:]
    for d, out in enumerate(outs):
        first = 0
        for got_ref, kept_ref in zip(ins[::2], ins[1::2]):
            last = first + got_ref.shape[1]
            out[first:last, :] = (got_ref[me ^ d].astype(F32) + kept_ref[me ^ d].astype(F32)).astype(BF16)
            first = last


def far_count(refs):
    return refs[0].shape[0]


def final_kernel(scale, *refs):
    parts, (conv_ref, res_ref) = refs[:-2], refs[-2:]
    total = parts[0][...].astype(F32)
    for ref in parts[1:]:
        total = total + ref[...].astype(F32)
    total = total * scale
    height = conv_ref.shape[0]
    conv_ref[...] = total[:height]
    res_ref[...] = total[height:]


def call(kernel, out_shapes, flops, *args, name, in_hbm=(), scratch=(), aliases=None):
    def spec(index, a):
        if index in in_hbm:
            return pl.BlockSpec(memory_space=pltpu.HBM)
        return pl.BlockSpec(memory_space=pltpu.SMEM if a.dtype == jnp.int32 else pltpu.VMEM)

    args = [pltpu.with_memory_space_constraint(a, pltpu.HBM) if i in in_hbm else a for i, a in enumerate(args)]
    out_shape = [jax.ShapeDtypeStruct(shape, kind) for shape, kind in out_shapes]
    moved = sum(a.size * a.dtype.itemsize for a in list(args) + out_shape)
    return pl.pallas_call(
        kernel,
        out_shape=out_shape,
        in_specs=[spec(i, a) for i, a in enumerate(args)],
        out_specs=[pl.BlockSpec(memory_space=pltpu.VMEM)] * len(out_shape),
        scratch_shapes=list(scratch),
        input_output_aliases=aliases or {},
        cost_estimate=pl.CostEstimate(flops=int(flops), bytes_accessed=int(moved), transcendentals=0),
        compiler_params=pltpu.CompilerParams(vmem_limit_bytes=VMEM_GRANT),
        name=name,
    )(*args)


def after(array, other):
    return lax.optimization_barrier((array, other))[0]


def body(samples, grad_out, w_conv, w_res, lengths):
    x, cot = samples[0], grad_out[0]
    rows, channels = x.shape
    step = DILATION_STEP
    tms, reps = lax.axis_size("tm"), lax.axis_size("rep")
    halves, count_z = tms // 2, reps // 2
    h, low = 2 * channels // tms, channels // reps
    lanes = channels // tms
    height = h + low
    devices = tms * reps
    product = 2 * rows * channels * channels

    def swap(array, mask):
        return lax.ppermute(array, ("tm", "rep"), [(i, i ^ mask) for i in range(devices)])

    halo = lax.ppermute(x[rows - step :], "tm", [(i, (i + 1) % tms) for i in range(tms)])
    whole_pg, whole_gb = ((rows, 2 * channels), BF16), ((tms, rows, lanes), BF16)
    xt, ct, cur, gg, pg, gb, wc, c_in = call(
        local_kernel,
        [
            ((tms // 2, h, rows), BF16), ((channels, rows), BF16), ((step, 2 * channels), F32),
            ((step, channels), F32), whole_pg, whole_gb, (w_conv.shape, BF16), (cot.shape, BF16),
        ],
        product * 4, lengths, x, cot, w_conv, w_res, name="local", in_hbm=(1, 2, 3, 4),
        scratch=[pltpu.VMEM(x.shape, BF16), pltpu.VMEM(w_res.shape, BF16), pltpu.SemaphoreType.DMA((5,))],
    )
    def core_of(device):
        return device // reps % 2

    def swap_mixed(array, first_mask, second_mask):
        return lax.ppermute(
            array, ("tm", "rep"), [(i, i ^ (second_mask if core_of(i) else first_mask)) for i in range(devices)]
        )

    fars = halves // 2 * count_z
    far_masks = [(d // count_z) * 4 * reps + (d % count_z) * 2 for d in range(fars)]
    core_mask, x_mask, y_mask = reps, 2 * reps, 1
    cut = (height * FIRST_CHUNK // 20) // 16 * 16
    sizes, starts = [cut, height - cut], [0, cut]
    terms = [((halves, reps, size, lanes), BF16) for size in sizes]
    pg, gb, ht, theirs = call(
        functools.partial(partner_kernel, starts[1]),
        [whole_pg, whole_gb, ((tms // 2, h, step), BF16), terms[1]],
        product * 3, lengths, halo, wc, xt, ct, cur, gg, pg, gb, name="partner", aliases={7: 0, 8: 1},
    )

    def terms_of(chunk, away):
        (out,) = call(
            functools.partial(terms_kernel, starts[chunk], away), [terms[chunk]], product * 2,
            xt, ht, ct, pg, gb, name=f"terms{chunk}{away}",
        )
        return out

    theirs = [terms_of(0, 1), theirs]
    got = [swap(part, core_mask) for part in theirs]
    sums = []
    for c, size in enumerate(sizes):
        stay, send = call(
            functools.partial(split_kernel, count_z), [((2 * fars, size, lanes), BF16)] * 2,
            halves * reps * size * lanes, got[c], terms_of(c, 0), name=f"split{c}",
        )
        sums.append((swap_mixed(send, x_mask, y_mask), stay))
    parts = []
    for c, size in enumerate(sizes):
        stay, send = call(
            functools.partial(half_kernel, count_z), [((fars, size, lanes), BF16)] * 2,
            2 * fars * size * lanes, *sums[c], name=f"half{c}",
        )
        parts += [swap_mixed(send, y_mask, x_mask), stay]
    (back,) = call(back_kernel, [((step, channels), BF16)], product, after(pg, parts[2]), wc, name="back")
    lo, hi = call(
        input_kernel, [((rows - step, channels), BF16), ((step, channels), F32)], product * 4,
        after(pg, sums[0][0]), wc, c_in, name="input",
    )
    outs = call(
        functools.partial(far_kernel, count_z), [((height, lanes), BF16)] * fars,
        fars * height * lanes, *parts, name="far",
    )
    arrived = lax.ppermute(back, "tm", [((i + 1) % tms, i) for i in range(tms)])
    parts = [swap(p, m) if m else p for p, m in zip(outs, far_masks)]
    parts = parts[:1:-1] + parts[:2]
    (grad_in,) = call(rows_kernel, [((rows, channels), BF16)], rows * channels, lo, hi, arrived, name="rows")
    scale = float(rows * devices) ** (-0.5)
    conv, res = call(
        functools.partial(final_kernel, scale),
        [((h, lanes), F32), ((low, lanes), F32)], height * lanes * 8, after(parts[0], grad_in), *parts[1:], name="final",
    )
    return grad_in[None], conv, res.T


def solution(mesh):
    return jax.shard_map(
        body,
        mesh=mesh,
        in_specs=(P("rep", "tm", None), P("rep", "tm", None), P(), P(), P("rep")),
        out_specs=(P("rep", "tm", None), P("tm", "rep"), P("tm", "rep")),
        check_vma=False,
    )
```

```python
import functools

import jax
import jax.numpy as jnp
from jax import lax
from jax.experimental import pallas as pl
from jax.experimental.pallas import tpu as pltpu
from jax.sharding import PartitionSpec as P

DILATION_STEP = 256
VMEM_GRANT = 32 * 1024 * 1024
FIRST_CHUNK = 10
F32, BF16 = jnp.float32, jnp.bfloat16


def dot(left, right):
    return jnp.dot(left, right, preferred_element_type=F32)


def dot_nt(left, right):
    return lax.dot_general(left, right, (((1,), (1,)), ((), ())), preferred_element_type=F32)


def gates(pre_act, gated_grad, in_length):
    channels = pre_act.shape[1] // 2
    tanh_f = jnp.tanh(pre_act[:, :channels])
    sig_g = 0.5 + 0.5 * jnp.tanh(0.5 * pre_act[:, channels:])
    both = tanh_f * sig_g
    gated = (in_length * both).astype(BF16)
    pre_f = (gated_grad * (sig_g * (1.0 - tanh_f * tanh_f))).astype(BF16)
    pre_g = (gated_grad * (both * (1.0 - sig_g))).astype(BF16)
    return gated, pre_f, pre_g


def length_mask(lengths_ref, first_row, rows, total_rows):
    start = lax.axis_index("tm") * total_rows + first_row
    at = start + lax.broadcasted_iota(jnp.int32, (rows, 1), 0)
    return (at < lengths_ref[0]).astype(F32)


def local_kernel(
    lengths_ref, x_hbm, c_hbm, wc_hbm, wr_hbm,
    xt_ref, ct_ref, cur_ref, gg_ref, pg_ref, gb_ref, wc_ref, c_ref, x_ref, wr_ref, sems,
):
    rows, channels = x_ref.shape
    step = DILATION_STEP
    lanes = gb_ref.shape[2]
    low, high = pl.ds(0, channels), pl.ds(channels, channels)
    copies = [
        pltpu.make_async_copy(source, target, sems.at[i])
        for i, (source, target) in enumerate(
            [
                (x_hbm, x_ref), (wc_hbm.at[high], wc_ref.at[high]), (wc_hbm.at[low], wc_ref.at[low]),
                (c_hbm, c_ref), (wr_hbm, wr_ref),
            ]
        )
    ]
    for copy in copies:
        copy.start()
    copies[0].wait()
    xt_ref[...] = x_ref[...].T.reshape(xt_ref.shape)
    copies[1].wait()
    cur_ref[...] = dot(x_ref[:step, :], wc_ref[channels:, :])
    pre_act = dot(x_ref[step:, :], wc_ref[channels:, :])
    copies[2].wait()
    pre_act = pre_act + dot(x_ref[: rows - step, :], wc_ref[:channels, :])
    copies[3].wait()
    copies[4].wait()
    gated_grad = dot_nt(c_ref[...], wr_ref[...])
    gg_ref[...] = gated_grad[:step] * length_mask(lengths_ref, 0, step, rows)
    mask = length_mask(lengths_ref, step, rows - step, rows)
    gated, pre_f, pre_g = gates(pre_act, gated_grad[step:] * mask, mask)
    for t in range(gb_ref.shape[0]):
        gb_ref[t, step:, :] = gated[:, t * lanes : (t + 1) * lanes]
    pg_ref[step:, :channels] = pre_f
    pg_ref[step:, channels:] = pre_g
    ct_ref[...] = c_ref[...].T


def block_products(first, parity, xt_ref, ht_ref, ct_ref, pg_ref, gb_ref, out_ref):
    halves, reps, size, lanes = out_ref.shape
    blocks, h, rows = xt_ref.shape
    back = ht_ref.shape[2]
    columns, channels = pg_ref.shape[1], ct_ref.shape[0]
    low, last = channels // reps, first + size
    count = min(last, h) - first
    if count > 0:
        some = pl.ds(first, count)
        picked = [2 * i + parity for i in range(blocks // 2)]
        earlier = [jnp.concatenate([ht_ref[i, some], xt_ref[i, some, : rows - back]], 1) for i in picked]
        left = jnp.concatenate(earlier + [xt_ref[i, some] for i in picked], 0)
        wide = min(256, columns)
        for j in range(0, columns, wide):
            term = dot(left, pg_ref[:, j : j + wide]).astype(BF16)
            for t in range(halves):
                for k in range(0, wide, lanes):
                    out_ref[t, (j + k) // lanes, :count, :] = term[t * count : (t + 1) * count, k : k + lanes]
    count = max(count, 0)
    if last > h:
        skip, part = max(first, h) - h, size - count
        right = jnp.concatenate([gb_ref[2 * t + parity] for t in range(halves)], 1)
        if part == low:
            left = ct_ref[...]
        else:
            left = jnp.concatenate([ct_ref[pl.ds(r * low + skip, part), :] for r in range(reps)], 0)
        term = dot(left, right).astype(BF16)
        for t in range(halves):
            for r in range(reps):
                out_ref[t, r, count:, :] = term[r * part : (r + 1) * part, t * lanes : (t + 1) * lanes]


def partner_kernel(
    first, lengths_ref, halo_ref, wc_ref, xt_ref, ct_ref, cur_ref, gg_ref, pg_in, gb_in,
    pg_ref, gb_ref, ht_ref, out_ref,
):
    step, channels = halo_ref.shape
    rows = pg_ref.shape[0]
    lanes = gb_ref.shape[2]
    halo = jnp.where(lax.axis_index("tm") > 0, halo_ref[...], jnp.zeros_like(halo_ref))
    pre_act = cur_ref[...] + dot(halo, wc_ref[:channels, :])
    mask = length_mask(lengths_ref, 0, step, rows)
    gated, pre_f, pre_g = gates(pre_act, gg_ref[...], mask)
    pg_ref[:step, :channels] = pre_f
    pg_ref[:step, channels:] = pre_g
    for t in range(gb_ref.shape[0]):
        gb_ref[t, :step, :] = gated[:, t * lanes : (t + 1) * lanes]
    ht_ref[...] = halo.T.reshape(ht_ref.shape)
    parity = 1 - lax.rem(lax.axis_index("tm"), 2)
    block_products(first, parity, xt_ref, ht_ref, ct_ref, pg_ref, gb_ref, out_ref)


def terms_kernel(first, away, xt_ref, ht_ref, ct_ref, pg_ref, gb_ref, out_ref):
    parity = lax.rem(lax.axis_index("tm") + away, 2)
    block_products(first, parity, xt_ref, ht_ref, ct_ref, pg_ref, gb_ref, out_ref)


def back_kernel(pg_ref, wc_ref, back_ref):
    step, channels = back_ref.shape
    back_ref[...] = dot_nt(pg_ref[:step, :], wc_ref[:channels, :]).astype(BF16)


def input_gradient(pg_ref, wc_ref, c_ref, lo_ref, hi_ref):
    step = DILATION_STEP
    rows, channels = c_ref.shape
    current = dot_nt(pg_ref[...], wc_ref[channels:, :]) + c_ref[...].astype(F32)
    earlier = dot_nt(pg_ref[step:, :], wc_ref[:channels, :])
    lo_ref[...] = (current[: rows - step] + earlier).astype(BF16)
    hi_ref[...] = current[rows - step :]


def input_kernel(pg_ref, wc_ref, c_ref, lo_in, hi_in, lo_ref, hi_ref):
    @pl.when(lax.rem(lax.axis_index("tm"), 2) == 0)
    def _():
        input_gradient(pg_ref, wc_ref, c_ref, lo_ref, hi_ref)


def rows_kernel(lo_ref, hi_ref, arrived_ref, out_ref):
    count = lo_ref.shape[0]
    arrived = jnp.where(lax.axis_index("tm") < lax.axis_size("tm") - 1, arrived_ref[...].astype(F32), 0.0)
    out_ref[:count, :] = lo_ref[...]
    out_ref[count:, :] = (hi_ref[...] + arrived).astype(BF16)


def coordinates(count_z):
    tm, rep = lax.axis_index("tm"), lax.axis_index("rep")
    return lax.rem(tm, 2), lax.rem(tm // 2, 2), lax.rem(rep, 2), (tm // 4) * count_z + rep // 2


def split_kernel(count_z, got_ref, kept_ref, stay_ref, send_ref):
    core, x, y, _ = coordinates(count_z)
    for s, out in enumerate((stay_ref, send_ref)):
        for j in range(out.shape[0]):
            far, other = j // 2, j % 2
            to_x = jnp.where(core == 0, x ^ s, other)
            to_y = jnp.where(core == 0, other, y ^ s)
            t, r = 2 * (far // count_z) + to_x, 2 * (far % count_z) + to_y
            out[j] = (got_ref[t, r].astype(F32) + kept_ref[t, r].astype(F32)).astype(BF16)


def half_kernel(count_z, got_ref, kept_ref, stay_ref, send_ref):
    core, x, y, _ = coordinates(count_z)
    mine = jnp.where(core == 0, y, x)
    for s, out in enumerate((stay_ref, send_ref)):
        for far in range(out.shape[0]):
            j = 2 * far + (mine ^ s)
            out[far] = (got_ref[j].astype(F32) + kept_ref[j].astype(F32)).astype(BF16)


def half_input_kernel(count_z, got_ref, kept_ref, pg_ref, wc_ref, c_ref, stay_ref, send_ref, lo_ref, hi_ref):
    @pl.when(lax.rem(lax.axis_index("tm"), 2) == 1)
    def _():
        input_gradient(pg_ref, wc_ref, c_ref, lo_ref, hi_ref)

    half_kernel(count_z, got_ref, kept_ref, stay_ref, send_ref)


def far_kernel(count_z, *refs):
    me = coordinates(count_z)[3]
    chunks = len(refs) - far_count(refs)
    ins, outs = refs[:chunks], refs[chunks:]
    for d, out in enumerate(outs):
        first = 0
        for got_ref, kept_ref in zip(ins[::2], ins[1::2]):
            last = first + got_ref.shape[1]
            out[first:last, :] = (got_ref[me ^ d].astype(F32) + kept_ref[me ^ d].astype(F32)).astype(BF16)
            first = last


def far_count(refs):
    return refs[0].shape[0]


def final_kernel(scale, *refs):
    parts, (conv_ref, res_ref) = refs[:-2], refs[-2:]
    total = parts[0][...].astype(F32)
    for ref in parts[1:]:
        total = total + ref[...].astype(F32)
    total = total * scale
    height = conv_ref.shape[0]
    conv_ref[...] = total[:height]
    res_ref[...] = total[height:]


def call(kernel, out_shapes, flops, *args, name, in_hbm=(), scratch=(), aliases=None):
    def spec(index, a):
        if index in in_hbm:
            return pl.BlockSpec(memory_space=pltpu.HBM)
        return pl.BlockSpec(memory_space=pltpu.SMEM if a.dtype == jnp.int32 else pltpu.VMEM)

    args = [pltpu.with_memory_space_constraint(a, pltpu.HBM) if i in in_hbm else a for i, a in enumerate(args)]
    out_shape = [jax.ShapeDtypeStruct(shape, kind) for shape, kind in out_shapes]
    moved = sum(a.size * a.dtype.itemsize for a in list(args) + out_shape)
    return pl.pallas_call(
        kernel,
        out_shape=out_shape,
        in_specs=[spec(i, a) for i, a in enumerate(args)],
        out_specs=[pl.BlockSpec(memory_space=pltpu.VMEM)] * len(out_shape),
        scratch_shapes=list(scratch),
        input_output_aliases=aliases or {},
        cost_estimate=pl.CostEstimate(flops=int(flops), bytes_accessed=int(moved), transcendentals=0),
        compiler_params=pltpu.CompilerParams(vmem_limit_bytes=VMEM_GRANT),
        name=name,
    )(*args)


def after(array, other):
    return lax.optimization_barrier((array, other))[0]


def body(samples, grad_out, w_conv, w_res, lengths):
    x, cot = samples[0], grad_out[0]
    rows, channels = x.shape
    step = DILATION_STEP
    tms, reps = lax.axis_size("tm"), lax.axis_size("rep")
    halves, count_z = tms // 2, reps // 2
    h, low = 2 * channels // tms, channels // reps
    lanes = channels // tms
    height = h + low
    devices = tms * reps
    product = 2 * rows * channels * channels

    def swap(array, mask):
        return lax.ppermute(array, ("tm", "rep"), [(i, i ^ mask) for i in range(devices)])

    halo = lax.ppermute(x[rows - step :], "tm", [(i, (i + 1) % tms) for i in range(tms)])
    whole_pg, whole_gb = ((rows, 2 * channels), BF16), ((tms, rows, lanes), BF16)
    xt, ct, cur, gg, pg, gb, wc, c_in = call(
        local_kernel,
        [
            ((tms // 2, h, rows), BF16), ((channels, rows), BF16), ((step, 2 * channels), F32),
            ((step, channels), F32), whole_pg, whole_gb, (w_conv.shape, BF16), (cot.shape, BF16),
        ],
        product * 4, lengths, x, cot, w_conv, w_res, name="local", in_hbm=(1, 2, 3, 4),
        scratch=[pltpu.VMEM(x.shape, BF16), pltpu.VMEM(w_res.shape, BF16), pltpu.SemaphoreType.DMA((5,))],
    )
    def core_of(device):
        return device // reps % 2

    def swap_mixed(array, first_mask, second_mask):
        return lax.ppermute(
            array, ("tm", "rep"), [(i, i ^ (second_mask if core_of(i) else first_mask)) for i in range(devices)]
        )

    fars = halves // 2 * count_z
    far_masks = [(d // count_z) * 4 * reps + (d % count_z) * 2 for d in range(fars)]
    core_mask, x_mask, y_mask = reps, 2 * reps, 1
    cut = (height * FIRST_CHUNK // 20) // 16 * 16
    sizes, starts = [cut, height - cut], [0, cut]
    terms = [((halves, reps, size, lanes), BF16) for size in sizes]
    pg, gb, ht, theirs = call(
        functools.partial(partner_kernel, starts[1]),
        [whole_pg, whole_gb, ((tms // 2, h, step), BF16), terms[1]],
        product * 3, lengths, halo, wc, xt, ct, cur, gg, pg, gb, name="partner", aliases={7: 0, 8: 1},
    )

    def terms_of(chunk, away):
        (out,) = call(
            functools.partial(terms_kernel, starts[chunk], away), [terms[chunk]], product * 2,
            xt, ht, ct, pg, gb, name=f"terms{chunk}{away}",
        )
        return out

    theirs = [terms_of(0, 1), theirs]
    got = [swap(part, core_mask) for part in theirs]
    sums = []
    for c, size in enumerate(sizes):
        stay, send = call(
            functools.partial(split_kernel, count_z), [((2 * fars, size, lanes), BF16)] * 2,
            halves * reps * size * lanes, got[c], terms_of(c, 0), name=f"split{c}",
        )
        sums.append((swap_mixed(send, x_mask, y_mask), stay))
    parts = []
    input_shapes = [((rows - step, channels), BF16), ((step, channels), F32)]
    for c, size in enumerate(sizes):
        if c == 1:
            stay, send, lo, hi = call(
                functools.partial(half_input_kernel, count_z), [((fars, size, lanes), BF16)] * 2 + input_shapes,
                2 * fars * size * lanes, *sums[c], pg, wc, c_in, name=f"half{c}",
            )
        else:
            stay, send = call(
                functools.partial(half_kernel, count_z), [((fars, size, lanes), BF16)] * 2,
                2 * fars * size * lanes, *sums[c], name=f"half{c}",
            )
        parts += [swap_mixed(send, y_mask, x_mask), stay]
    (back,) = call(back_kernel, [((step, channels), BF16)], product, after(pg, parts[2]), wc, name="back")
    lo, hi = call(input_kernel, input_shapes, product * 4, pg, wc, c_in, lo, hi, name="input", aliases={3: 0, 4: 1})
    outs = call(
        functools.partial(far_kernel, count_z), [((height, lanes), BF16)] * fars,
        fars * height * lanes, *parts, name="far",
    )
    arrived = lax.ppermute(back, "tm", [((i + 1) % tms, i) for i in range(tms)])
    parts = [swap(p, m) if m else p for p, m in zip(outs, far_masks)]
    parts = parts[:1:-1] + parts[:2]
    (grad_in,) = call(rows_kernel, [((rows, channels), BF16)], rows * channels, lo, hi, arrived, name="rows")
    scale = float(rows * devices) ** (-0.5)
    conv, res = call(
        functools.partial(final_kernel, scale),
        [((h, lanes), F32), ((low, lanes), F32)], height * lanes * 8, after(parts[0], grad_in), *parts[1:], name="final",
    )
    return grad_in[None], conv, res.T


def solution(mesh):
    return jax.shard_map(
        body,
        mesh=mesh,
        in_specs=(P("rep", "tm", None), P("rep", "tm", None), P(), P(), P("rep")),
        out_specs=(P("rep", "tm", None), P("tm", "rep"), P("tm", "rep")),
        check_vma=False,
    )
```

```python
import functools

import jax
import jax.numpy as jnp
from jax import lax
from jax.experimental import pallas as pl
from jax.experimental.pallas import tpu as pltpu
from jax.sharding import PartitionSpec as P

DILATION_STEP = 256
VMEM_GRANT = 32 * 1024 * 1024
FIRST_CHUNK = 10
F32, BF16 = jnp.float32, jnp.bfloat16


def dot(left, right):
    return jnp.dot(left, right, preferred_element_type=F32)


def dot_nt(left, right):
    return lax.dot_general(left, right, (((1,), (1,)), ((), ())), preferred_element_type=F32)


def gates(pre_act, gated_grad, in_length):
    channels = pre_act.shape[1] // 2
    tanh_f = jnp.tanh(pre_act[:, :channels])
    sig_g = 0.5 + 0.5 * jnp.tanh(0.5 * pre_act[:, channels:])
    both = tanh_f * sig_g
    gated = (in_length * both).astype(BF16)
    pre_f = (gated_grad * (sig_g * (1.0 - tanh_f * tanh_f))).astype(BF16)
    pre_g = (gated_grad * (both * (1.0 - sig_g))).astype(BF16)
    return gated, pre_f, pre_g


def length_mask(lengths_ref, first_row, rows, total_rows):
    start = lax.axis_index("tm") * total_rows + first_row
    at = start + lax.broadcasted_iota(jnp.int32, (rows, 1), 0)
    return (at < lengths_ref[0]).astype(F32)


def local_kernel(
    lengths_ref, x_hbm, c_hbm, wc_hbm, wr_hbm,
    xt_ref, ct_ref, cur_ref, gg_ref, pg_ref, gb_ref, wc_ref, c_ref, x_ref, wr_ref, sems,
):
    rows, channels = x_ref.shape
    step = DILATION_STEP
    lanes = gb_ref.shape[2]
    low, high = pl.ds(0, channels), pl.ds(channels, channels)
    copies = [
        pltpu.make_async_copy(source, target, sems.at[i])
        for i, (source, target) in enumerate(
            [
                (x_hbm, x_ref), (wc_hbm.at[high], wc_ref.at[high]), (wc_hbm.at[low], wc_ref.at[low]),
                (c_hbm, c_ref), (wr_hbm, wr_ref),
            ]
        )
    ]
    for copy in copies:
        copy.start()
    copies[0].wait()
    xt_ref[...] = x_ref[...].T.reshape(xt_ref.shape)
    copies[1].wait()
    cur_ref[...] = dot(x_ref[:step, :], wc_ref[channels:, :])
    pre_act = dot(x_ref[step:, :], wc_ref[channels:, :])
    copies[2].wait()
    pre_act = pre_act + dot(x_ref[: rows - step, :], wc_ref[:channels, :])
    copies[3].wait()
    copies[4].wait()
    gated_grad = dot_nt(c_ref[...], wr_ref[...])
    gg_ref[...] = gated_grad[:step] * length_mask(lengths_ref, 0, step, rows)
    mask = length_mask(lengths_ref, step, rows - step, rows)
    gated, pre_f, pre_g = gates(pre_act, gated_grad[step:] * mask, mask)
    for t in range(gb_ref.shape[0]):
        gb_ref[t, step:, :] = gated[:, t * lanes : (t + 1) * lanes]
    pg_ref[step:, :channels] = pre_f
    pg_ref[step:, channels:] = pre_g
    ct_ref[...] = c_ref[...].T


def block_products(first, parity, xt_ref, ht_ref, ct_ref, pg_ref, gb_ref, out_ref):
    halves, reps, size, lanes = out_ref.shape
    blocks, h, rows = xt_ref.shape
    back = ht_ref.shape[2]
    columns, channels = pg_ref.shape[1], ct_ref.shape[0]
    low, last = channels // reps, first + size
    count = min(last, h) - first
    if count > 0:
        some = pl.ds(first, count)
        picked = [2 * i + parity for i in range(blocks // 2)]
        earlier = [jnp.concatenate([ht_ref[i, some], xt_ref[i, some, : rows - back]], 1) for i in picked]
        left = jnp.concatenate(earlier + [xt_ref[i, some] for i in picked], 0)
        wide = min(512, columns)
        for j in range(0, columns, wide):
            term = dot(left, pg_ref[:, j : j + wide]).astype(BF16)
            for t in range(halves):
                for k in range(0, wide, lanes):
                    out_ref[t, (j + k) // lanes, :count, :] = term[t * count : (t + 1) * count, k : k + lanes]
    count = max(count, 0)
    if last > h:
        skip, part = max(first, h) - h, size - count
        right = jnp.concatenate([gb_ref[2 * t + parity] for t in range(halves)], 1)
        if part == low:
            left = ct_ref[...]
        else:
            left = jnp.concatenate([ct_ref[pl.ds(r * low + skip, part), :] for r in range(reps)], 0)
        term = dot(left, right).astype(BF16)
        for t in range(halves):
            for r in range(reps):
                out_ref[t, r, count:, :] = term[r * part : (r + 1) * part, t * lanes : (t + 1) * lanes]


def partner_kernel(
    first, lengths_ref, halo_ref, wc_ref, xt_ref, ct_ref, cur_ref, gg_ref, pg_in, gb_in,
    pg_ref, gb_ref, ht_ref, out_ref,
):
    step, channels = halo_ref.shape
    rows = pg_ref.shape[0]
    lanes = gb_ref.shape[2]
    halo = jnp.where(lax.axis_index("tm") > 0, halo_ref[...], jnp.zeros_like(halo_ref))
    pre_act = cur_ref[...] + dot(halo, wc_ref[:channels, :])
    mask = length_mask(lengths_ref, 0, step, rows)
    gated, pre_f, pre_g = gates(pre_act, gg_ref[...], mask)
    pg_ref[:step, :channels] = pre_f
    pg_ref[:step, channels:] = pre_g
    for t in range(gb_ref.shape[0]):
        gb_ref[t, :step, :] = gated[:, t * lanes : (t + 1) * lanes]
    ht_ref[...] = halo.T.reshape(ht_ref.shape)
    parity = 1 - lax.rem(lax.axis_index("tm"), 2)
    block_products(first, parity, xt_ref, ht_ref, ct_ref, pg_ref, gb_ref, out_ref)


def terms_kernel(first, away, xt_ref, ht_ref, ct_ref, pg_ref, gb_ref, out_ref):
    parity = lax.rem(lax.axis_index("tm") + away, 2)
    block_products(first, parity, xt_ref, ht_ref, ct_ref, pg_ref, gb_ref, out_ref)


def back_product(pg_ref, wc_ref, back_ref):
    step, channels = back_ref.shape
    back_ref[...] = dot_nt(pg_ref[:step, :], wc_ref[:channels, :]).astype(BF16)


def back_kernel(pg_ref, wc_ref, back_in, back_ref):
    @pl.when(lax.rem(lax.axis_index("tm"), 2) == 0)
    def _():
        back_product(pg_ref, wc_ref, back_ref)


def input_gradient(pg_ref, wc_ref, c_ref, lo_ref, hi_ref):
    step = DILATION_STEP
    rows, channels = c_ref.shape
    current = dot_nt(pg_ref[...], wc_ref[channels:, :]) + c_ref[...].astype(F32)
    earlier = dot_nt(pg_ref[step:, :], wc_ref[:channels, :])
    lo_ref[...] = (current[: rows - step] + earlier).astype(BF16)
    hi_ref[...] = current[rows - step :]


def input_kernel(pg_ref, wc_ref, c_ref, lo_in, hi_in, lo_ref, hi_ref):
    @pl.when(lax.rem(lax.axis_index("tm"), 2) == 0)
    def _():
        input_gradient(pg_ref, wc_ref, c_ref, lo_ref, hi_ref)


def rows_kernel(lo_ref, hi_ref, arrived_ref, out_ref):
    count = lo_ref.shape[0]
    arrived = jnp.where(lax.axis_index("tm") < lax.axis_size("tm") - 1, arrived_ref[...].astype(F32), 0.0)
    out_ref[:count, :] = lo_ref[...]
    out_ref[count:, :] = (hi_ref[...] + arrived).astype(BF16)


def coordinates(count_z):
    tm, rep = lax.axis_index("tm"), lax.axis_index("rep")
    return lax.rem(tm, 2), lax.rem(tm // 2, 2), lax.rem(rep, 2), (tm // 4) * count_z + rep // 2


def split_kernel(count_z, got_ref, kept_ref, stay_ref, send_ref):
    core, x, y, _ = coordinates(count_z)
    for s, out in enumerate((stay_ref, send_ref)):
        for j in range(out.shape[0]):
            far, other = j // 2, j % 2
            to_x = jnp.where(core == 0, x ^ s, other)
            to_y = jnp.where(core == 0, other, y ^ s)
            t, r = 2 * (far // count_z) + to_x, 2 * (far % count_z) + to_y
            out[j] = (got_ref[t, r].astype(F32) + kept_ref[t, r].astype(F32)).astype(BF16)


def half_kernel(count_z, got_ref, kept_ref, stay_ref, send_ref):
    core, x, y, _ = coordinates(count_z)
    mine = jnp.where(core == 0, y, x)
    for s, out in enumerate((stay_ref, send_ref)):
        for far in range(out.shape[0]):
            j = 2 * far + (mine ^ s)
            out[far] = (got_ref[j].astype(F32) + kept_ref[j].astype(F32)).astype(BF16)


def half_input_kernel(count_z, got_ref, kept_ref, pg_ref, wc_ref, c_ref, stay_ref, send_ref, lo_ref, hi_ref, back_ref):
    @pl.when(lax.rem(lax.axis_index("tm"), 2) == 1)
    def _():
        input_gradient(pg_ref, wc_ref, c_ref, lo_ref, hi_ref)
        back_product(pg_ref, wc_ref, back_ref)

    half_kernel(count_z, got_ref, kept_ref, stay_ref, send_ref)


def far_kernel(count_z, *refs):
    me = coordinates(count_z)[3]
    chunks = len(refs) - far_count(refs)
    ins, outs = refs[:chunks], refs[chunks:]
    for d, out in enumerate(outs):
        first = 0
        for got_ref, kept_ref in zip(ins[::2], ins[1::2]):
            last = first + got_ref.shape[1]
            out[first:last, :] = (got_ref[me ^ d].astype(F32) + kept_ref[me ^ d].astype(F32)).astype(BF16)
            first = last


def far_count(refs):
    return refs[0].shape[0]


def final_kernel(scale, *refs):
    parts, (conv_ref, res_ref) = refs[:-2], refs[-2:]
    total = parts[0][...].astype(F32)
    for ref in parts[1:]:
        total = total + ref[...].astype(F32)
    total = total * scale
    height = conv_ref.shape[0]
    conv_ref[...] = total[:height]
    res_ref[...] = total[height:]


def call(kernel, out_shapes, flops, *args, name, in_hbm=(), scratch=(), aliases=None):
    def spec(index, a):
        if index in in_hbm:
            return pl.BlockSpec(memory_space=pltpu.HBM)
        return pl.BlockSpec(memory_space=pltpu.SMEM if a.dtype == jnp.int32 else pltpu.VMEM)

    args = [pltpu.with_memory_space_constraint(a, pltpu.HBM) if i in in_hbm else a for i, a in enumerate(args)]
    out_shape = [jax.ShapeDtypeStruct(shape, kind) for shape, kind in out_shapes]
    moved = sum(a.size * a.dtype.itemsize for a in list(args) + out_shape)
    return pl.pallas_call(
        kernel,
        out_shape=out_shape,
        in_specs=[spec(i, a) for i, a in enumerate(args)],
        out_specs=[pl.BlockSpec(memory_space=pltpu.VMEM)] * len(out_shape),
        scratch_shapes=list(scratch),
        input_output_aliases=aliases or {},
        cost_estimate=pl.CostEstimate(flops=int(flops), bytes_accessed=int(moved), transcendentals=0),
        compiler_params=pltpu.CompilerParams(vmem_limit_bytes=VMEM_GRANT),
        name=name,
    )(*args)


def after(array, other):
    return lax.optimization_barrier((array, other))[0]


def body(samples, grad_out, w_conv, w_res, lengths):
    x, cot = samples[0], grad_out[0]
    rows, channels = x.shape
    step = DILATION_STEP
    tms, reps = lax.axis_size("tm"), lax.axis_size("rep")
    halves, count_z = tms // 2, reps // 2
    h, low = 2 * channels // tms, channels // reps
    lanes = channels // tms
    height = h + low
    devices = tms * reps
    product = 2 * rows * channels * channels

    def swap(array, mask):
        return lax.ppermute(array, ("tm", "rep"), [(i, i ^ mask) for i in range(devices)])

    halo = lax.ppermute(x[rows - step :], "tm", [(i, (i + 1) % tms) for i in range(tms)])
    whole_pg, whole_gb = ((rows, 2 * channels), BF16), ((tms, rows, lanes), BF16)
    xt, ct, cur, gg, pg, gb, wc, c_in = call(
        local_kernel,
        [
            ((tms // 2, h, rows), BF16), ((channels, rows), BF16), ((step, 2 * channels), F32),
            ((step, channels), F32), whole_pg, whole_gb, (w_conv.shape, BF16), (cot.shape, BF16),
        ],
        product * 4, lengths, x, cot, w_conv, w_res, name="local", in_hbm=(1, 2, 3, 4),
        scratch=[pltpu.VMEM(x.shape, BF16), pltpu.VMEM(w_res.shape, BF16), pltpu.SemaphoreType.DMA((5,))],
    )
    def core_of(device):
        return device // reps % 2

    def swap_mixed(array, first_mask, second_mask):
        return lax.ppermute(
            array, ("tm", "rep"), [(i, i ^ (second_mask if core_of(i) else first_mask)) for i in range(devices)]
        )

    fars = halves // 2 * count_z
    far_masks = [(d // count_z) * 4 * reps + (d % count_z) * 2 for d in range(fars)]
    core_mask, x_mask, y_mask = reps, 2 * reps, 1
    cut = (height * FIRST_CHUNK // 20) // 16 * 16
    sizes, starts = [cut, height - cut], [0, cut]
    terms = [((halves, reps, size, lanes), BF16) for size in sizes]
    pg, gb, ht, theirs = call(
        functools.partial(partner_kernel, starts[1]),
        [whole_pg, whole_gb, ((tms // 2, h, step), BF16), terms[1]],
        product * 3, lengths, halo, wc, xt, ct, cur, gg, pg, gb, name="partner", aliases={7: 0, 8: 1},
    )

    def terms_of(chunk, away):
        (out,) = call(
            functools.partial(terms_kernel, starts[chunk], away), [terms[chunk]], product * 2,
            xt, ht, ct, pg, gb, name=f"terms{chunk}{away}",
        )
        return out

    theirs = [terms_of(0, 1), theirs]
    got = [swap(part, core_mask) for part in theirs]
    sums = []
    for c, size in enumerate(sizes):
        stay, send = call(
            functools.partial(split_kernel, count_z), [((2 * fars, size, lanes), BF16)] * 2,
            halves * reps * size * lanes, got[c], terms_of(c, 0), name=f"split{c}",
        )
        sums.append((swap_mixed(send, x_mask, y_mask), stay))
    parts = []
    input_shapes = [((rows - step, channels), BF16), ((step, channels), F32)]
    for c, size in enumerate(sizes):
        if c == 1:
            stay, send, lo, hi, back = call(
                functools.partial(half_input_kernel, count_z), [((fars, size, lanes), BF16)] * 2 + input_shapes + [((step, channels), BF16)],
                2 * fars * size * lanes, *sums[c], pg, wc, c_in, name=f"half{c}",
            )
        else:
            stay, send = call(
                functools.partial(half_kernel, count_z), [((fars, size, lanes), BF16)] * 2,
                2 * fars * size * lanes, *sums[c], name=f"half{c}",
            )
        parts += [swap_mixed(send, y_mask, x_mask), stay]
    (back,) = call(back_kernel, [((step, channels), BF16)], product, after(pg, parts[2]), wc, back, name="back", aliases={2: 0})
    lo, hi = call(input_kernel, input_shapes, product * 4, pg, wc, c_in, lo, hi, name="input", aliases={3: 0, 4: 1})
    outs = call(
        functools.partial(far_kernel, count_z), [((height, lanes), BF16)] * fars,
        fars * height * lanes, *parts, name="far",
    )
    arrived = lax.ppermute(back, "tm", [((i + 1) % tms, i) for i in range(tms)])
    parts = [swap(p, m) if m else p for p, m in zip(outs, far_masks)]
    parts = parts[:1:-1] + parts[:2]
    (grad_in,) = call(rows_kernel, [((rows, channels), BF16)], rows * channels, lo, hi, arrived, name="rows")
    scale = float(rows * devices) ** (-0.5)
    conv, res = call(
        functools.partial(final_kernel, scale),
        [((h, lanes), F32), ((low, lanes), F32)], height * lanes * 8, after(parts[0], grad_in), *parts[1:], name="final",
    )
    return grad_in[None], conv, res.T


def solution(mesh):
    return jax.shard_map(
        body,
        mesh=mesh,
        in_specs=(P("rep", "tm", None), P("rep", "tm", None), P(), P(), P("rep")),
        out_specs=(P("rep", "tm", None), P("tm", "rep"), P("tm", "rep")),
        check_vma=False,
    )
```

```python
import functools

import jax
import jax.numpy as jnp
from jax import lax
from jax.experimental import pallas as pl
from jax.experimental.pallas import tpu as pltpu
from jax.sharding import PartitionSpec as P

DILATION_STEP = 256
VMEM_GRANT = 32 * 1024 * 1024
FIRST_CHUNK = 10
F32, BF16 = jnp.float32, jnp.bfloat16


def dot(left, right):
    return jnp.dot(left, right, preferred_element_type=F32)


def dot_nt(left, right):
    return lax.dot_general(left, right, (((1,), (1,)), ((), ())), preferred_element_type=F32)


def gates(pre_act, gated_grad, in_length):
    channels = pre_act.shape[1] // 2
    tanh_f = jnp.tanh(pre_act[:, :channels])
    sig_g = 0.5 + 0.5 * jnp.tanh(0.5 * pre_act[:, channels:])
    both = tanh_f * sig_g
    gated = (in_length * both).astype(BF16)
    pre_f = (gated_grad * (sig_g * (1.0 - tanh_f * tanh_f))).astype(BF16)
    pre_g = (gated_grad * (both * (1.0 - sig_g))).astype(BF16)
    return gated, pre_f, pre_g


def length_mask(lengths_ref, first_row, rows, total_rows):
    start = lax.axis_index("tm") * total_rows + first_row
    at = start + lax.broadcasted_iota(jnp.int32, (rows, 1), 0)
    return (at < lengths_ref[0]).astype(F32)


def local_kernel(
    lengths_ref, x_hbm, c_hbm, wc_hbm, wr_hbm,
    xt_ref, ct_ref, cur_ref, gg_ref, pg_ref, gb_ref, wc_ref, c_ref, x_ref, wr_ref, sems,
):
    rows, channels = x_ref.shape
    step = DILATION_STEP
    lanes = gb_ref.shape[2]
    low, high = pl.ds(0, channels), pl.ds(channels, channels)
    copies = [
        pltpu.make_async_copy(source, target, sems.at[i])
        for i, (source, target) in enumerate(
            [
                (x_hbm, x_ref), (wc_hbm.at[high], wc_ref.at[high]), (wc_hbm.at[low], wc_ref.at[low]),
                (c_hbm, c_ref), (wr_hbm, wr_ref),
            ]
        )
    ]
    for copy in copies:
        copy.start()
    copies[0].wait()
    xt_ref[...] = x_ref[...].T.reshape(xt_ref.shape)
    copies[1].wait()
    cur_ref[...] = dot(x_ref[:step, :], wc_ref[channels:, :])
    pre_act = dot(x_ref[step:, :], wc_ref[channels:, :])
    copies[2].wait()
    pre_act = pre_act + dot(x_ref[: rows - step, :], wc_ref[:channels, :])
    copies[3].wait()
    copies[4].wait()
    gated_grad = dot_nt(c_ref[...], wr_ref[...])
    gg_ref[...] = gated_grad[:step] * length_mask(lengths_ref, 0, step, rows)
    mask = length_mask(lengths_ref, step, rows - step, rows)
    gated, pre_f, pre_g = gates(pre_act, gated_grad[step:] * mask, mask)
    for t in range(gb_ref.shape[0]):
        gb_ref[t, step:, :] = gated[:, t * lanes : (t + 1) * lanes]
    pg_ref[step:, :channels] = pre_f
    pg_ref[step:, channels:] = pre_g
    ct_ref[...] = c_ref[...].T


def block_products(first, parity, xt_ref, ht_ref, ct_ref, pg_ref, gb_ref, out_ref):
    halves, reps, size, lanes = out_ref.shape
    blocks, h, rows = xt_ref.shape
    back = ht_ref.shape[2]
    columns, channels = pg_ref.shape[1], ct_ref.shape[0]
    low, last = channels // reps, first + size
    count = min(last, h) - first
    if count > 0:
        some = pl.ds(first, count)
        picked = [2 * i + parity for i in range(blocks // 2)]
        earlier = [jnp.concatenate([ht_ref[i, some], xt_ref[i, some, : rows - back]], 1) for i in picked]
        left = jnp.concatenate(earlier + [xt_ref[i, some] for i in picked], 0)
        wide = min(512, columns)
        for j in range(0, columns, wide):
            term = dot(left, pg_ref[:, j : j + wide]).astype(BF16)
            for t in range(halves):
                for k in range(0, wide, lanes):
                    out_ref[t, (j + k) // lanes, :count, :] = term[t * count : (t + 1) * count, k : k + lanes]
    count = max(count, 0)
    if last > h:
        skip, part = max(first, h) - h, size - count
        right = jnp.concatenate([gb_ref[2 * t + parity] for t in range(halves)], 1)
        if part == low:
            left = ct_ref[...]
        else:
            left = jnp.concatenate([ct_ref[pl.ds(r * low + skip, part), :] for r in range(reps)], 0)
        term = dot(left, right).astype(BF16)
        for t in range(halves):
            for r in range(reps):
                out_ref[t, r, count:, :] = term[r * part : (r + 1) * part, t * lanes : (t + 1) * lanes]


def partner_kernel(
    first, lengths_ref, halo_ref, wc_ref, xt_ref, ct_ref, cur_ref, gg_ref, pg_in, gb_in,
    pg_ref, gb_ref, ht_ref, out_ref,
):
    step, channels = halo_ref.shape
    rows = pg_ref.shape[0]
    lanes = gb_ref.shape[2]
    halo = jnp.where(lax.axis_index("tm") > 0, halo_ref[...], jnp.zeros_like(halo_ref))
    pre_act = cur_ref[...] + dot(halo, wc_ref[:channels, :])
    mask = length_mask(lengths_ref, 0, step, rows)
    gated, pre_f, pre_g = gates(pre_act, gg_ref[...], mask)
    pg_ref[:step, :channels] = pre_f
    pg_ref[:step, channels:] = pre_g
    for t in range(gb_ref.shape[0]):
        gb_ref[t, :step, :] = gated[:, t * lanes : (t + 1) * lanes]
    ht_ref[...] = halo.T.reshape(ht_ref.shape)
    parity = 1 - lax.rem(lax.axis_index("tm"), 2)
    block_products(first, parity, xt_ref, ht_ref, ct_ref, pg_ref, gb_ref, out_ref)


def terms_kernel(first, away, xt_ref, ht_ref, ct_ref, pg_ref, gb_ref, out_ref):
    parity = lax.rem(lax.axis_index("tm") + away, 2)
    block_products(first, parity, xt_ref, ht_ref, ct_ref, pg_ref, gb_ref, out_ref)


def back_product(pg_ref, wc_ref, back_ref):
    step, channels = back_ref.shape
    back_ref[...] = dot_nt(pg_ref[:step, :], wc_ref[:channels, :]).astype(BF16)


def back_kernel(pg_ref, wc_ref, back_in, back_ref):
    @pl.when(lax.rem(lax.axis_index("tm"), 2) == 0)
    def _():
        back_product(pg_ref, wc_ref, back_ref)


def input_gradient(pg_ref, wc_ref, c_ref, lo_ref, hi_ref):
    step = DILATION_STEP
    rows, channels = c_ref.shape
    current = dot_nt(pg_ref[...], wc_ref[channels:, :]) + c_ref[...].astype(F32)
    earlier = dot_nt(pg_ref[step:, :], wc_ref[:channels, :])
    lo_ref[...] = (current[: rows - step] + earlier).astype(BF16)
    hi_ref[...] = current[rows - step :]


def input_kernel(pg_ref, wc_ref, c_ref, lo_in, hi_in, lo_ref, hi_ref):
    @pl.when(lax.rem(lax.axis_index("tm"), 2) == 0)
    def _():
        input_gradient(pg_ref, wc_ref, c_ref, lo_ref, hi_ref)


def rows_kernel(lo_ref, hi_ref, arrived_ref, out_ref):
    count = lo_ref.shape[0]
    arrived = jnp.where(lax.axis_index("tm") < lax.axis_size("tm") - 1, arrived_ref[...].astype(F32), 0.0)
    out_ref[:count, :] = lo_ref[...]
    out_ref[count:, :] = (hi_ref[...] + arrived).astype(BF16)


def coordinates(count_z):
    tm, rep = lax.axis_index("tm"), lax.axis_index("rep")
    return lax.rem(tm, 2), lax.rem(tm // 2, 2), lax.rem(rep, 2), (tm // 4) * count_z + rep // 2


def split_kernel(count_z, got_ref, kept_ref, stay_ref, send_ref):
    core, x, y, _ = coordinates(count_z)
    for s, out in enumerate((stay_ref, send_ref)):
        for j in range(out.shape[0]):
            far, other = j // 2, j % 2
            to_x = jnp.where(core == 0, x ^ s, other)
            to_y = jnp.where(core == 0, other, y ^ s)
            t, r = 2 * (far // count_z) + to_x, 2 * (far % count_z) + to_y
            out[j] = (got_ref[t, r].astype(F32) + kept_ref[t, r].astype(F32)).astype(BF16)


def half_kernel(count_z, got_ref, kept_ref, stay_ref, send_ref):
    core, x, y, _ = coordinates(count_z)
    mine = jnp.where(core == 0, y, x)
    for s, out in enumerate((stay_ref, send_ref)):
        for far in range(out.shape[0]):
            j = 2 * far + (mine ^ s)
            out[far] = (got_ref[j].astype(F32) + kept_ref[j].astype(F32)).astype(BF16)


def half_input_kernel(count_z, got_ref, kept_ref, pg_ref, wc_ref, c_ref, stay_ref, send_ref, lo_ref, hi_ref, back_ref):
    @pl.when(lax.rem(lax.axis_index("tm"), 2) == 1)
    def _():
        input_gradient(pg_ref, wc_ref, c_ref, lo_ref, hi_ref)
        back_product(pg_ref, wc_ref, back_ref)

    half_kernel(count_z, got_ref, kept_ref, stay_ref, send_ref)


def far_kernel(count_z, *refs):
    me = coordinates(count_z)[3]
    chunks = len(refs) - far_count(refs)
    ins, outs = refs[:chunks], refs[chunks:]
    for d, out in enumerate(outs):
        first, to = 0, lax.rem(me + d, len(outs))
        for got_ref, kept_ref in zip(ins[::2], ins[1::2]):
            last = first + got_ref.shape[1]
            out[first:last, :] = (got_ref[to].astype(F32) + kept_ref[to].astype(F32)).astype(BF16)
            first = last


def far_count(refs):
    return refs[0].shape[0]


def final_kernel(scale, *refs):
    parts, (conv_ref, res_ref) = refs[:-2], refs[-2:]
    total = parts[0][...].astype(F32)
    for ref in parts[1:]:
        total = total + ref[...].astype(F32)
    total = total * scale
    height = conv_ref.shape[0]
    conv_ref[...] = total[:height]
    res_ref[...] = total[height:]


def call(kernel, out_shapes, flops, *args, name, in_hbm=(), scratch=(), aliases=None):
    def spec(index, a):
        if index in in_hbm:
            return pl.BlockSpec(memory_space=pltpu.HBM)
        return pl.BlockSpec(memory_space=pltpu.SMEM if a.dtype == jnp.int32 else pltpu.VMEM)

    args = [pltpu.with_memory_space_constraint(a, pltpu.HBM) if i in in_hbm else a for i, a in enumerate(args)]
    out_shape = [jax.ShapeDtypeStruct(shape, kind) for shape, kind in out_shapes]
    moved = sum(a.size * a.dtype.itemsize for a in list(args) + out_shape)
    return pl.pallas_call(
        kernel,
        out_shape=out_shape,
        in_specs=[spec(i, a) for i, a in enumerate(args)],
        out_specs=[pl.BlockSpec(memory_space=pltpu.VMEM)] * len(out_shape),
        scratch_shapes=list(scratch),
        input_output_aliases=aliases or {},
        cost_estimate=pl.CostEstimate(flops=int(flops), bytes_accessed=int(moved), transcendentals=0),
        compiler_params=pltpu.CompilerParams(vmem_limit_bytes=VMEM_GRANT),
        name=name,
    )(*args)


def after(array, other):
    return lax.optimization_barrier((array, other))[0]


def body(samples, grad_out, w_conv, w_res, lengths):
    x, cot = samples[0], grad_out[0]
    rows, channels = x.shape
    step = DILATION_STEP
    tms, reps = lax.axis_size("tm"), lax.axis_size("rep")
    halves, count_z = tms // 2, reps // 2
    h, low = 2 * channels // tms, channels // reps
    lanes = channels // tms
    height = h + low
    devices = tms * reps
    product = 2 * rows * channels * channels

    def swap(array, mask):
        return lax.ppermute(array, ("tm", "rep"), [(i, i ^ mask) for i in range(devices)])

    halo = lax.ppermute(x[rows - step :], "tm", [(i, (i + 1) % tms) for i in range(tms)])
    whole_pg, whole_gb = ((rows, 2 * channels), BF16), ((tms, rows, lanes), BF16)
    xt, ct, cur, gg, pg, gb, wc, c_in = call(
        local_kernel,
        [
            ((tms // 2, h, rows), BF16), ((channels, rows), BF16), ((step, 2 * channels), F32),
            ((step, channels), F32), whole_pg, whole_gb, (w_conv.shape, BF16), (cot.shape, BF16),
        ],
        product * 4, lengths, x, cot, w_conv, w_res, name="local", in_hbm=(1, 2, 3, 4),
        scratch=[pltpu.VMEM(x.shape, BF16), pltpu.VMEM(w_res.shape, BF16), pltpu.SemaphoreType.DMA((5,))],
    )
    def core_of(device):
        return device // reps % 2

    def swap_mixed(array, first_mask, second_mask):
        return lax.ppermute(
            array, ("tm", "rep"), [(i, i ^ (second_mask if core_of(i) else first_mask)) for i in range(devices)]
        )

    fars = halves // 2 * count_z
    core_mask, x_mask, y_mask = reps, 2 * reps, 1
    cut = (height * FIRST_CHUNK // 20) // 16 * 16
    sizes, starts = [cut, height - cut], [0, cut]
    terms = [((halves, reps, size, lanes), BF16) for size in sizes]
    pg, gb, ht, theirs = call(
        functools.partial(partner_kernel, starts[1]),
        [whole_pg, whole_gb, ((tms // 2, h, step), BF16), terms[1]],
        product * 3, lengths, halo, wc, xt, ct, cur, gg, pg, gb, name="partner", aliases={7: 0, 8: 1},
    )

    def terms_of(chunk, away):
        (out,) = call(
            functools.partial(terms_kernel, starts[chunk], away), [terms[chunk]], product * 2,
            xt, ht, ct, pg, gb, name=f"terms{chunk}{away}",
        )
        return out

    theirs = [terms_of(0, 1), theirs]
    got = [swap(part, core_mask) for part in theirs]
    sums = []
    for c, size in enumerate(sizes):
        stay, send = call(
            functools.partial(split_kernel, count_z), [((2 * fars, size, lanes), BF16)] * 2,
            halves * reps * size * lanes, got[c], terms_of(c, 0), name=f"split{c}",
        )
        sums.append((swap_mixed(send, x_mask, y_mask), stay))
    parts = []
    input_shapes = [((rows - step, channels), BF16), ((step, channels), F32)]
    for c, size in enumerate(sizes):
        if c == 1:
            stay, send, lo, hi, back = call(
                functools.partial(half_input_kernel, count_z), [((fars, size, lanes), BF16)] * 2 + input_shapes + [((step, channels), BF16)],
                2 * fars * size * lanes, *sums[c], pg, wc, c_in, name=f"half{c}",
            )
        else:
            stay, send = call(
                functools.partial(half_kernel, count_z), [((fars, size, lanes), BF16)] * 2,
                2 * fars * size * lanes, *sums[c], name=f"half{c}",
            )
        parts += [swap_mixed(send, y_mask, x_mask), stay]
    (back,) = call(back_kernel, [((step, channels), BF16)], product, after(pg, parts[2]), wc, back, name="back", aliases={2: 0})
    lo, hi = call(input_kernel, input_shapes, product * 4, pg, wc, c_in, lo, hi, name="input", aliases={3: 0, 4: 1})
    outs = call(
        functools.partial(far_kernel, count_z), [((height, lanes), BF16)] * fars,
        fars * height * lanes, *parts, name="far",
    )
    arrived = lax.ppermute(back, "tm", [((i + 1) % tms, i) for i in range(tms)])
    def shifted(array, by):
        pairs = []
        for i in range(devices):
            tm, rep = divmod(i, reps)
            far = (tm // 4 * count_z + rep // 2 + by) % fars
            pairs.append((i, (far // count_z * 4 + tm % 4) * reps + far % count_z * 2 + rep % 2))
        return lax.ppermute(array, ("tm", "rep"), pairs)

    parts = [shifted(p, d) if d else p for d, p in enumerate(outs)]
    parts = parts[1:] + parts[:1]
    (grad_in,) = call(rows_kernel, [((rows, channels), BF16)], rows * channels, lo, hi, arrived, name="rows")
    scale = float(rows * devices) ** (-0.5)
    conv, res = call(
        functools.partial(final_kernel, scale),
        [((h, lanes), F32), ((low, lanes), F32)], height * lanes * 8, after(parts[0], grad_in), *parts[1:], name="final",
    )
    return grad_in[None], conv, res.T


def solution(mesh):
    return jax.shard_map(
        body,
        mesh=mesh,
        in_specs=(P("rep", "tm", None), P("rep", "tm", None), P(), P(), P("rep")),
        out_specs=(P("rep", "tm", None), P("tm", "rep"), P("tm", "rep")),
        check_vma=False,
    )
```
